32 devices in a mesh: dp: 8 (over z, y), tensor: 4 (over x, core).
Axes of the slice: x: 2, y: 2, z: 4, core: 2. Of those that a mesh axis runs over, the one named last changes fastest.
Arguments:
- layer_input: bfloat16 [4096, 2560], P(('dp', 'tensor')), may hold values from -6 to 6
- doc_ids: int32 [4096], P('dp'), may hold values from 0 to 4, as said below
- norm_in: bfloat16 [2, 2560], P(None, 'dp'), may hold values from 0.5 to 1.5
- q_down: bfloat16 [2, 2560, 768], P(None, 'dp'), may hold values from -0.125 to 0.125
- q_gain: bfloat16 [2, 768], P(None, 'dp'), may hold values from 0.5 to 1.5
- q_up: bfloat16 [2, 768, 3840], P(None, 'dp', 'tensor'), may hold values from -0.21875 to 0.21875
- kv_down: bfloat16 [2, 2560, 288], P(None, 'dp'), may hold values from -0.125 to 0.125
- kv_gain: bfloat16 [2, 256], P(None, 'dp'), may hold values from 0.5 to 1.5
- kv_up: bfloat16 [2, 256, 5120], P(None, 'dp', 'tensor'), may hold values from -0.375 to 0.375
- out_proj: bfloat16 [2, 2560, 2560], P(None, 'tensor', 'dp'), may hold values from -2 to 2
- norm_post: bfloat16 [2, 2560], P(None, 'dp'), may hold values from 0.5 to 1.5
- gate_proj: bfloat16 [2, 2560, 6400], P(None, 'dp', 'tensor'), may hold values from -0.125 to 0.125
- up_proj: bfloat16 [2, 2560, 6400], P(None, 'dp', 'tensor'), may hold values from -0.125 to 0.125
- down_proj: bfloat16 [2, 6400, 2560], P(None, 'tensor', 'dp'), may hold values from -0.375 to 0.375
- out_grad: bfloat16 [4096, 2560], P(('dp', 'tensor')), may hold values from -6 to 6
Outputs:
- layer_output: bfloat16 [4096, 2560], P(('dp', 'tensor'))
- input_grad: bfloat16 [4096, 2560], P(('dp', 'tensor'))
- grad_norm_in: float32 [2, 2560], P(None, 'dp')
- grad_q_down: float32 [2, 2560, 768], P(None, 'dp')
- grad_q_gain: float32 [2, 768], P(None, 'dp')
- grad_q_up: float32 [2, 768, 3840], P(None, 'dp', 'tensor')
- grad_kv_down: float32 [2, 2560, 288], P(None, 'dp')
- grad_kv_gain: float32 [2, 256], P(None, 'dp')
- grad_kv_up: float32 [2, 256, 5120], P(None, 'dp', 'tensor')
- grad_out_proj: float32 [2, 2560, 2560], P(None, 'tensor', 'dp')
- grad_norm_post: float32 [2, 2560], P(None, 'dp')
- grad_gate_proj: float32 [2, 2560, 6400], P(None, 'dp', 'tensor')
- grad_up_proj: float32 [2, 2560, 6400], P(None, 'dp', 'tensor')
- grad_down_proj: float32 [2, 6400, 2560], P(None, 'tensor', 'dp')
The draws below stay inside these ranges and needn't reach their ends.
Inputs may be any that keep to these rules, and one draw needn't show every extreme that they name: `doc_ids`: within each group of 512 rows (one index of dp) the ids start at 0 and rise by 0 or 1 from row to row, ending at 4; rows with equal ids form one document.
All inputs are finite; a program needn't handle non-finite values.
Results may differ from the reference program's by a relative error of at most 0.035.
Values may be sent and summed in bfloat16 or wider, within the bound.
No kernel may reach another device: no remote copies, remote signals or barrier semaphores. Data moves between devices by JAX's collectives and lax.ppermute only.
A program may use at most 320 MiB of HBM per device.

```python
import math
import jax
import jax.numpy as jnp
from jax import lax

D = 2560
H = 40
NOPE = 64
ROPE = 32
VDIM = 64
QR = 768
KVR = 256
FF = 6400
LAYERS = 2
TOK_DEV = 128
QK = 96
ROWS = 512
TOKENS = 4096


def group_documents(source_key):
    first_key, second_key, third_key, fourth_key = jax.random.split(source_key, 4)
    first_row = jax.random.randint(first_key, (), 2, TOK_DEV)
    tail_rows = jax.random.randint(second_key, (), 2, TOK_DEV)
    stop_row = ROWS - tail_rows
    left_split = jax.random.randint(third_key, (), 1, first_row)
    right_split = stop_row + jax.random.randint(fourth_key, (), 1, tail_rows)
    places = jnp.arange(ROWS, dtype=jnp.int32)
    marks = ((places == left_split) | (places == first_row) | (places == stop_row) | (places == right_split)).astype(jnp.int32)
    return jnp.cumsum(marks).astype(jnp.int32)


def draw_doc_ids(key, part):
    key = jax.random.fold_in(key, 17)
    groups = TOKENS // ROWS
    return jax.vmap(group_documents)(jax.random.split(key, groups)).reshape(TOKENS)


def block_scale(rng, dims, pieces, least, high):
    def one(position, parts):
        heights = jax.random.uniform(jax.random.fold_in(jax.random.fold_in(rng, 6), position), (parts,), jnp.float32, least / len(pieces), high / len(pieces))
        return jnp.repeat(jnp.exp(heights), dims[position] // parts).reshape((-1,) + (1,) * (len(dims) - position - 1))

    level = one(*pieces[0])
    for cut in pieces[1:]:
        level = level * one(*cut)
    return level


def centred(stream_key, shape, deviation, reach, pieces=(), kind=jnp.bfloat16):
    array = deviation * jax.random.normal(stream_key, shape, jnp.float32)
    if pieces:
        array = array * block_scale(stream_key, shape, pieces, -0.22, 0.18)
    return jnp.clip(array, -reach, reach).astype(kind)


def setup_inputs(seed: int = 0) -> dict:
    streams_of = jax.random.split(jax.random.key(seed), 16)
    layer_input = centred(streams_of[0], (TOKENS, D), 1.0, 6.0, ((0, 32),))
    doc_ids = draw_doc_ids(jax.random.fold_in(streams_of[15], 71), 0)
    norm_in = jnp.clip(1.0 + 0.1 * jax.random.normal(streams_of[2], (LAYERS, D), jnp.float32), 0.5, 1.5).astype(jnp.bfloat16)
    q_down = centred(streams_of[3], (LAYERS, D, QR), D ** -0.5, 0.125, ((1, 8),))
    q_gain = jnp.clip(1.0 + 0.1 * jax.random.normal(streams_of[4], (LAYERS, QR), jnp.float32), 0.5, 1.5).astype(jnp.bfloat16)
    q_up = centred(streams_of[5], (LAYERS, QR, H * QK), QR ** -0.5, 0.21875, ((1, 8), (2, 4)))
    kv_down = centred(streams_of[6], (LAYERS, D, KVR + ROPE), D ** -0.5, 0.125, ((1, 8),))
    kv_gain = jnp.clip(1.0 + 0.1 * jax.random.normal(streams_of[7], (LAYERS, KVR), jnp.float32), 0.5, 1.5).astype(jnp.bfloat16)
    kv_up = centred(streams_of[8], (LAYERS, KVR, H * (NOPE + VDIM)), KVR ** -0.5, 0.375, ((1, 8), (2, 4)))
    out_proj = centred(streams_of[9], (LAYERS, H * VDIM, D), (max(H * VDIM // 320, 1)) ** -0.5, 2.0, ((1, 4), (2, 8)))
    norm_post = jnp.clip(1.0 + 0.1 * jax.random.normal(streams_of[10], (LAYERS, D), jnp.float32), 0.5, 1.5).astype(jnp.bfloat16)
    gate_proj = centred(streams_of[11], (LAYERS, D, FF), D ** -0.5, 0.125, ((1, 8), (2, 4)))
    up_proj = centred(streams_of[12], (LAYERS, D, FF), D ** -0.5, 0.125, ((1, 8), (2, 4)))
    down_proj = centred(streams_of[13], (LAYERS, FF, D), (max(FF // 25, 1)) ** -0.5, 0.375, ((1, 4), (2, 8)))
    out_grad = centred(streams_of[14], (TOKENS, D), 1.0, 6.0, ((0, 32),))
    return dict(layer_input=layer_input, doc_ids=doc_ids, norm_in=norm_in, q_down=q_down, q_gain=q_gain, q_up=q_up, kv_down=kv_down, kv_gain=kv_gain, kv_up=kv_up, out_proj=out_proj, norm_post=norm_post, gate_proj=gate_proj, up_proj=up_proj, down_proj=down_proj, out_grad=out_grad)


epsilon = 1e-05
residual_scale = 1.4 / math.sqrt(62.0)
rope_base = 10000.0
masked_score = -1e+30

@jax.custom_vjp
def low(v):
    return lax.optimization_barrier(v.astype(jnp.bfloat16)).astype(jnp.float32)

@jax.custom_vjp
def low_back(v):
    return v

def low_keep(v):
    return (low(v), None)

def low_pass(kept, grad):
    return (grad,)

def back_keep(v):
    return (v, None)

def back_low(kept, grad):
    return (low(grad),)
low.defvjp(low_keep, low_pass)
low_back.defvjp(back_keep, back_low)

def matmul(left, right):
    return jnp.dot(left, right, precision=lax.Precision.HIGHEST)

def norm_rows(values, gain):
    return values * lax.rsqrt(lax.optimization_barrier(jnp.mean(values * values, axis=-1, keepdims=True)) + epsilon) * gain

def rotate(rotary, cosine, sine_table):
    half_width = rotary.shape[-1] // 2
    first_half = rotary[..., :half_width]
    second_half = rotary[..., half_width:]
    return jnp.concatenate([first_half * cosine - second_half * sine_table, second_half * cosine + first_half * sine_table], axis=-1)

def tables(doc_ids):
    groups = doc_ids.shape[0] // ROWS
    grouped = doc_ids.reshape(groups, ROWS)
    places = jnp.arange(ROWS, dtype=jnp.int32)
    begins = jnp.concatenate([jnp.ones((groups, 1), dtype=bool), grouped[:, 1:] != grouped[:, :-1]], axis=1)
    starts = lax.cummax(jnp.where(begins, places[None, :], 0), axis=1)
    positions = (places[None, :] - starts).reshape(-1).astype(jnp.float32)
    frequency = rope_base ** (-jnp.arange(0, ROPE, 2, dtype=jnp.float32) / ROPE)
    angles = positions[:, None] * frequency[None, :]
    return (jnp.cos(angles), jnp.sin(angles))

def attend(inputs):
    queries, key_rows, values, group_ids = inputs
    places = jnp.arange(ROWS, dtype=jnp.int32)
    allowed = (group_ids[:, None] == group_ids[None, :]) & (places[:, None] >= places[None, :])
    scores = jnp.einsum('qhd,khd->hqk', queries, key_rows, precision=lax.Precision.HIGHEST) * (1.0 / math.sqrt(QK))
    scores = jnp.where(allowed[None], low_back(scores), masked_score)
    probability = jax.nn.softmax(scores, axis=-1)
    return jnp.einsum('hqk,khd->qhd', low(probability), values, precision=lax.Precision.HIGHEST)

def one_layer(rows_in, weights, cosine, sine_table, doc_ids):
    gain_in, q_down_w, q_gain_w, q_up_w, kv_down_w, kv_gain_w, kv_up_w, out_w, gain_post, gate_w, up_w, down_w = weights
    rows_total = rows_in.shape[0]
    groups = rows_total // ROWS
    normed_in = low(norm_rows(rows_in, gain_in))
    q_latent = low_back(matmul(normed_in, q_down_w))
    q_normed = low(norm_rows(q_latent, q_gain_w))
    q_full = low_back(matmul(q_normed, q_up_w)).reshape(rows_total, H, QK)
    kv_latent = low_back(matmul(normed_in, kv_down_w))
    kv_normed = low(norm_rows(kv_latent[:, :KVR], kv_gain_w))
    kv_full = low_back(matmul(kv_normed, kv_up_w)).reshape(rows_total, H, NOPE + VDIM)
    queries = low(jnp.concatenate([q_full[..., :NOPE], rotate(q_full[..., NOPE:], cosine[:, None, :], sine_table[:, None, :])], axis=-1))
    shared = rotate(kv_latent[:, KVR:], cosine, sine_table)
    key_rows = low(jnp.concatenate([kv_full[..., :NOPE], jnp.broadcast_to(shared[:, None, :], (rows_total, H, ROPE))], axis=-1))
    values = low(kv_full[..., NOPE:])
    attended = lax.map(jax.checkpoint(attend), (queries.reshape(groups, ROWS, H, QK), key_rows.reshape(groups, ROWS, H, QK), values.reshape(groups, ROWS, H, VDIM), doc_ids.reshape(groups, ROWS)))
    attended = low(low_back(attended.reshape(rows_total, H * VDIM)))
    middle = rows_in + residual_scale * low_back(matmul(attended, out_w))
    normed_mid = low(norm_rows(middle, gain_post))
    gate_act = low_back(matmul(normed_mid, gate_w))
    up_act = low_back(matmul(normed_mid, up_w))
    hidden = low(jax.nn.silu(gate_act) * up_act)
    return middle + residual_scale * low_back(matmul(hidden, down_w))

def reference(layer_input, doc_ids, norm_in, q_down, q_gain, q_up, kv_down, kv_gain, kv_up, out_proj, norm_post, gate_proj, up_proj, down_proj, out_grad):
    stacks = tuple((weight_stack.astype(jnp.float32) for weight_stack in (norm_in, q_down, q_gain, q_up, kv_down, kv_gain, kv_up, out_proj, norm_post, gate_proj, up_proj, down_proj)))
    cosine, sine_table = tables(doc_ids)

    def forward(start_rows, weight_stacks):
        current = start_rows
        for layer_index in range(LAYERS):
            current = one_layer(current, tuple((weight_stack[layer_index] for weight_stack in weight_stacks)), cosine, sine_table, doc_ids)
        return current
    result, pullback = jax.vjp(forward, layer_input.astype(jnp.float32), stacks)
    grad_rows, grad_stacks = pullback(out_grad.astype(jnp.float32))
    return (result.astype(jnp.bfloat16), grad_rows.astype(jnp.bfloat16), grad_stacks[0], grad_stacks[1], grad_stacks[2], grad_stacks[3], grad_stacks[4], grad_stacks[5], grad_stacks[6], grad_stacks[7], grad_stacks[8], grad_stacks[9], grad_stacks[10], grad_stacks[11])
```

```python
import functools
import math

import jax
import jax.numpy as jnp
from jax import lax
from jax.sharding import PartitionSpec as P

NOPE = 64
ROPE = 32
VDIM = 64
QR = 768
KVR = 256
LAYERS = 2
QK = 96

epsilon = 1e-05
residual_scale = 1.4 / math.sqrt(62.0)
rope_base = 10000.0
masked_score = -1e30
bf16 = jnp.bfloat16
f32 = jnp.float32

plan = {
    "doc": (0, 3),
    "gains": (0, 1, 2, 3),
    "s": (0, 1, 2),
    "a0": (0, 1, 3),
    "g0": (1, 2, 3, 5, 6),
    "u0": (2, 4, 5, 6, 7),
    "d0": (3, 4, 6, 7, 8),
    "w1": (2, 3, 4, 5),
    "a1": (5, 6, 7, 9),
    "g1": (5, 6, 9, 11, 12),
    "u1": (6, 7, 11, 12, 13),
    "d1": (6, 7, 12, 13, 14),
    "w0": (12, 13, 14, 15),
    "grad d1": (15, 16, 17, 18),
    "grad g1": (16, 17, 18, 19),
    "grad u1": (17, 19, 21, 22),
    "grad a1": (19, 21, 23, 24),
    "grad s1": (21, 22, 23, 24),
    "grad gains1": (20, 21, 22, 23, 24),
    "grad d0": (22, 23, 24, 25),
    "grad g0": (23, 24, 26, 27),
    "grad u0": (24, 26, 27),
    "grad a0": (26, 27),
}

PAIR = 2


def dot(left, right, left_dim, right_dim):
    return lax.dot_general(
        left, right, (((left_dim,), (right_dim,)), ((), ())), preferred_element_type=f32
    )


def norm_parts(values):
    inverse = lax.rsqrt(jnp.mean(values * values, axis=-1, keepdims=True) + epsilon)
    return (values * inverse, inverse)


def norm_back(normed, inverse, gain, upstream):
    scaled = upstream * gain
    result = inverse * (scaled - normed * jnp.mean(scaled * normed, axis=-1, keepdims=True))
    return (result, jnp.sum(upstream * normed, axis=0))


def rotate(rotary, cosine, sine_table):
    half_width = rotary.shape[-1] // 2
    first_half = rotary[..., :half_width]
    second_half = rotary[..., half_width:]
    return jnp.concatenate(
        [
            first_half * cosine - second_half * sine_table,
            second_half * cosine + first_half * sine_table,
        ],
        axis=-1,
    )


def rotate_back(upstream, cosine, sine_table):
    return rotate(upstream, cosine, -sine_table)


class Flow:
    def __init__(self, plan, swap):
        self.plan = plan
        self.swap = swap
        self.count = -1
        self.work = {}
        self.due = {}
        self.results = {}

    def add(self, name, steps):
        self.work[name] = (steps, next(steps), None)
        self.due[name] = list(self.plan.get(name, ()))

    def begin(self, name, steps, request):
        moving = [a if axis is None else self.swap(a, axis, bit) for a, axis, bit in request]
        self.work[name] = (steps, None, moving)

    def advance(self, name, steps, arrived):
        try:
            request = steps.send(arrived)
        except StopIteration as end:
            self.results[name] = end.value
            del self.work[name]
            return
        self.begin(name, steps, request)

    def tick(self, *values):
        self.count += 1
        now = []
        for name in self.work:
            due = self.due[name]
            if due and due[0] <= self.count:
                due.pop(0)
                now.append(name)
        held = []
        for name in now:
            _, request, moving = self.work[name]
            held.append([a for a, _, _ in request] if moving is None else moving)
        flat = [a for arrays in held for a in arrays]
        values = list(values)
        if flat:
            out = lax.optimization_barrier((*values, *flat))
            values, flat = list(out[: len(values)]), list(out[len(values) :])
        for name, arrays in zip(now, held):
            tied, flat = flat[: len(arrays)], flat[len(arrays) :]
            steps, request, moving = self.work[name]
            if moving is None:
                self.begin(name, steps, [(a, *r[1:]) for a, r in zip(tied, request)])
            else:
                self.advance(name, steps, tied)
        return values[0] if len(values) == 1 else values

    def result(self, name):
        while name in self.work:
            steps, request, moving = self.work[name]
            if moving is None:
                self.begin(name, steps, request)
            else:
                self.advance(name, steps, moving)
        return self.results[name]


class Place:
    def __init__(self, dp, tensor):
        self.flow = Flow(plan, self.swap)
        self.dp = dp
        self.tensor = tensor
        self.group_bits = [1 << j for j in reversed(range(dp.bit_length() - 1)) if 1 << j != PAIR]
        self.pieces = dp // 2
        self.here = lax.axis_index("dp")
        self.column = lax.axis_index("tensor")
        self.low = (self.here & PAIR) == 0
        self.pairs = [
            [(base | pair * PAIR) * tensor + t for pair in range(2) for t in range(tensor)]
            for base in range(dp)
            if not base & PAIR
        ]

    def swap(self, array, axis, bit):
        size = self.dp if axis == "dp" else self.tensor
        return lax.ppermute(array, axis, [(i, i ^ bit) for i in range(size)])

    def relative(self, piece):
        return sum(bit for j, bit in enumerate(self.group_bits) if piece >> j & 1)

    def order(self):
        return [
            (self.relative(piece) | pair * PAIR)
            for piece in range(self.pieces)
            for pair in range(2)
        ]

    def flip(self, blocks):
        for bit in self.group_bits:
            own = (self.here & bit) != 0
            blocks = [jnp.where(own, blocks[k ^ bit], blocks[k]) for k in range(self.dp)]
        return blocks

    def to_group(self, array, axis):
        blocks = self.flip(jnp.split(array, self.dp, axis=axis))
        return jnp.concatenate([blocks[k] for k in self.order()], axis=axis)

    def from_group(self, array, axis):
        parts = jnp.split(array, self.dp, axis=axis)
        blocks = [None] * self.dp
        for part, k in zip(parts, self.order()):
            blocks[k] = part
        return jnp.concatenate(self.flip(blocks), axis=axis)

    def gather_all(self, array):
        blocks = array[None]
        for j in range(self.dp.bit_length() - 1):
            (taken,) = yield [(blocks, "dp", 1 << j)]
            blocks = jnp.concatenate([blocks, taken], axis=0)
        blocks = [blocks[k] for k in range(self.dp)]
        for j in range(self.dp.bit_length() - 1):
            own = (self.here & (1 << j)) != 0
            blocks = [jnp.where(own, blocks[k ^ (1 << j)], blocks[k]) for k in range(self.dp)]
        return jnp.stack(blocks)

    def gather_weight(self, prepare, *arrays):
        if arrays:
            arrays = yield [(a, None, 0) for a in arrays]
        low, high = prepare(*arrays)
        mine = jnp.where(self.low, low, high)
        (taken,) = yield [(jnp.where(self.low, high, low), "dp", PAIR)]
        pieces = [
            jnp.concatenate(
                [jnp.where(self.low, mine, taken), jnp.where(self.low, taken, mine)], axis=0
            )
        ]
        pieces = yield from self.gather_pieces(pieces)
        return jnp.concatenate(pieces, axis=0)

    def gather_pieces(self, pieces):
        total = len(self.group_bits)
        held = {0: pieces[0]}
        for moves in range(1, total + 1):
            wanted = [k for k in range(1 << total) if k.bit_count() == moves]
            taken = yield [
                (held[k & ~(1 << j)], "dp", self.group_bits[j])
                for k in wanted
                for j in [k.bit_length() - 1]
            ]
            held.update(zip(wanted, taken))
        return [held[k] for k in range(1 << total)]

    def scatter_grad(self, prepare, *arrays):
        if arrays:
            arrays = yield [(a, None, 0) for a in arrays]
        send, keep = prepare(*arrays)
        for bit in reversed(self.group_bits):
            (taken,) = yield [(send, "dp", bit)]
            total = (keep.astype(f32) + taken.astype(f32)).astype(bf16)
            keep, send = jnp.split(total, 2, axis=0)
        (taken,) = yield [(jnp.where(self.low, send, keep), "dp", PAIR)]
        mine = jnp.where(self.low, keep, send)
        return jnp.where(self.low, mine, taken), jnp.where(self.low, taken, mine)

    def gather_whole(self, share):
        (share,) = yield [(share, None, 0)]
        pieces = yield from self.gather_pieces([share])
        joined = self.gather_rows(jnp.concatenate(pieces, axis=0), tiled=False)
        rows, columns = share.shape
        joined = joined.reshape(2, self.tensor, self.pieces, rows, columns)
        return joined.transpose(2, 0, 1, 3, 4).reshape(-1, columns)

    def sum_all(self, blocks):
        blocks = [blocks[k] for k in range(self.dp)]
        bits = [1 << j for j in range(self.dp.bit_length() - 1)]
        for bit in bits:
            own = (self.here & bit) != 0
            blocks = [jnp.where(own, blocks[k ^ bit], blocks[k]) for k in range(self.dp)]
        total = jnp.stack(blocks)
        for bit in reversed(bits):
            half = total.shape[0] // 2
            (taken,) = yield [(total[half:], "dp", bit)]
            total = total[:half] + taken
        for bit in (1, 2):
            (taken,) = yield [(total, "tensor", bit)]
            total = total + taken
        return total[0]

    def gather_rows(self, rows, tiled=True):
        return lax.all_gather(
            rows, ("dp", "tensor"), axis=0, tiled=tiled, axis_index_groups=self.pairs
        )

    def relative_rows(self, rows):
        count = rows.shape[0] // (2 * self.tensor)
        own = jnp.where(self.low, 0, self.tensor) + self.column

        def half(core):
            return jnp.concatenate(
                [
                    lax.dynamic_slice_in_dim(
                        rows, (own ^ (pair * self.tensor + across * 2 + core)) * count, count, 0
                    )
                    for pair in range(2)
                    for across in range(2)
                ],
                axis=0,
            )

        return half(0), half(1)

    def scatter_rows(self, own, other):
        count = own.shape[0] // 4
        half = count // 2
        taken = self.swap(other, "tensor", 1)
        total = (own.astype(f32) + taken.astype(f32)).astype(bf16)
        rows, across, along = total[:count], total[count : 2 * count], total[2 * count : 3 * count]
        corner_first = self.swap(total[3 * count : 3 * count + half], "dp", PAIR)
        corner_second = self.swap(total[3 * count + half :], "tensor", 2)
        across = jnp.concatenate(
            [(across[:half].astype(f32) + corner_first.astype(f32)).astype(bf16), across[half:]],
            axis=0,
        )
        along = jnp.concatenate(
            [along[:half], (along[half:].astype(f32) + corner_second.astype(f32)).astype(bf16)],
            axis=0,
        )
        across = self.swap(across, "tensor", 2)
        along = self.swap(along, "dp", PAIR)
        return rows.astype(f32) + across.astype(f32) + along.astype(f32)

    def own_rows(self, rows):
        count = rows.shape[0] // (2 * self.tensor)
        own = jnp.where(self.low, 0, self.tensor) + self.column
        return lax.dynamic_slice_in_dim(rows, own * count, count, 0)

    def in_order(self, array, axis, bit, place_axis):
        taken = self.swap(array, axis, bit)
        index = self.here if axis == "dp" else self.column
        first = (index & bit) == 0
        return jnp.stack(
            [jnp.where(first, array, taken), jnp.where(first, taken, array)], axis=place_axis
        )


def tables(docs):
    rows_total = docs.shape[1]
    spots = jnp.arange(rows_total, dtype=jnp.int32)
    same = docs[:, :, None] == docs[:, None, :]
    allowed = same & (spots[:, None] >= spots[None, :])
    starts = jnp.sum((docs[:, None, :] < docs[:, :, None]).astype(jnp.int32), axis=-1)
    positions = (spots[None, :] - starts).astype(f32)
    frequency = rope_base ** (-jnp.arange(0, ROPE, 2, dtype=f32) / ROPE)
    angles = positions[..., None] * frequency
    return (jnp.cos(angles), jnp.sin(angles), allowed)


def scores_of(queries, key_rows, allowed):
    scores = jnp.einsum("bqhd,bkhd->bhqk", queries, key_rows, preferred_element_type=f32)
    return jnp.where(allowed[:, None], scores * (1.0 / math.sqrt(QK)), masked_score)


def attend_forward(queries, key_rows, values, allowed):
    scores = scores_of(queries, key_rows, allowed)
    highest = jnp.max(scores, axis=-1, keepdims=True)
    expanded = jnp.exp(scores - highest)
    totals = jnp.sum(expanded, axis=-1, keepdims=True)
    probs_low = (expanded / totals).astype(bf16)
    attended = jnp.einsum("bhqk,bkhd->bqhd", probs_low, values, preferred_element_type=f32)
    return (attended, highest + jnp.log(totals))


def attend_backward(queries, key_rows, values, allowed, log_totals, att_grad):
    scale_factor = 1.0 / math.sqrt(QK)
    probability = jnp.exp(scores_of(queries, key_rows, allowed) - log_totals)
    probs_low = probability.astype(bf16)
    value_grad = jnp.einsum("bhqk,bqhd->bkhd", probs_low, att_grad, preferred_element_type=f32)
    prob_grad = jnp.einsum("bqhd,bkhd->bhqk", att_grad, values, preferred_element_type=f32)
    inner_sum = jnp.sum(prob_grad * probability, axis=-1, keepdims=True)
    score_grad = (probability * (prob_grad - inner_sum)).astype(bf16)
    query_grad = (
        jnp.einsum("bhqk,bkhd->bqhd", score_grad, key_rows, preferred_element_type=f32)
        * scale_factor
    )
    key_grad = (
        jnp.einsum("bhqk,bqhd->bkhd", score_grad, queries, preferred_element_type=f32)
        * scale_factor
    )
    return query_grad, key_grad, value_grad


def rotate_own(place, array, cosine, sine_table):
    flat = (-1, cosine.shape[-1])
    return rotate(
        array, place.own_rows(cosine.reshape(flat)), place.own_rows(sine_table.reshape(flat))
    )


def first_latents(place, shares, cosine, sine_table, gains):
    _, _, q_gain, kv_gain, _ = gains
    width = QR // shares.shape[0]
    rows_total = shares.shape[1]
    q_latent = jnp.swapaxes(shares[..., :width], 0, 1).reshape(rows_total, -1).astype(f32)
    kv_latent = jnp.swapaxes(shares[..., width:], 0, 1).reshape(rows_total, -1).astype(f32)
    q_normed, q_inverse = norm_parts(q_latent)
    kv_normed, kv_inverse = norm_parts(kv_latent[:, :KVR])
    flat = (-1, cosine.shape[-1])
    shared = rotate(kv_latent[:, KVR:], cosine.reshape(flat), sine_table.reshape(flat))
    latents = jnp.concatenate([q_normed * q_gain, kv_normed * kv_gain, shared], axis=1)
    own = [place.own_rows(v) for v in (q_normed, q_inverse, kv_normed, kv_inverse)]
    return latents.astype(bf16), own


def own_latents(place, low_in, down_latent, cosine, sine_table, gains):
    _, _, q_gain, kv_gain, _ = gains
    latent = dot(low_in, down_latent, 1, 0)
    q_normed, q_inverse = norm_parts(latent[:, :QR])
    kv_normed, kv_inverse = norm_parts(latent[:, QR : QR + KVR])
    shared = rotate_own(place, latent[:, QR + KVR :], cosine, sine_table)
    packed = jnp.concatenate([q_normed * q_gain, kv_normed * kv_gain, shared], axis=1).astype(bf16)
    return packed, [q_normed, q_inverse, kv_normed, kv_inverse]


def layer_forward(place, layer, rows_in, latents, cosine, sine_table, allowed, gains):
    flow = place.flow
    gain_post = gains[4]
    group_rows = allowed.shape[1]
    q_up, kv_up, out_t = flow.result(f"a{layer}")
    latents, q_up, kv_up, out_t = flow.tick(latents, q_up, kv_up, out_t)
    heads = q_up.shape[1] // QK
    q_low = latents[:, :QR]
    kv_low = latents[:, QR : QR + KVR]
    q_full = dot(q_low, q_up, 1, 0).reshape(2, group_rows, heads, QK)
    kv_full = dot(kv_low, kv_up, 1, 0).reshape(2, group_rows, heads, NOPE + VDIM)
    queries = jnp.concatenate(
        [
            q_full[..., :NOPE],
            rotate(q_full[..., NOPE:], cosine[:, :, None, :], sine_table[:, :, None, :]),
        ],
        axis=-1,
    ).astype(bf16)
    key_rows = jnp.concatenate(
        [
            kv_full[..., :NOPE].astype(bf16),
            jnp.broadcast_to(
                latents[:, QR + KVR :].reshape(2, group_rows, 1, ROPE),
                (2, group_rows, heads, ROPE),
            ),
        ],
        axis=-1,
    )
    values = kv_full[..., NOPE:].astype(bf16)
    attended, log_totals = attend_forward(queries, key_rows, values, allowed)
    att_low = attended.reshape(2 * group_rows, heads * VDIM).astype(bf16)
    att_low = flow.tick(att_low)
    att_own, att_other = place.relative_rows(att_low)
    middle = rows_in + residual_scale * place.scatter_rows(
        dot(att_own, out_t, 1, 1).astype(bf16), dot(att_other, out_t, 1, 1).astype(bf16)
    )
    middle = flow.tick(middle)
    normed_mid, inv_mid = norm_parts(middle)
    all_mid = place.gather_rows((normed_mid * gain_post).astype(bf16))
    all_mid = flow.tick(all_mid)
    gate = flow.result(f"g{layer}")
    up = flow.result(f"u{layer}")
    gate_act = dot(all_mid, gate, 1, 0)
    up_act = dot(all_mid, up, 1, 0)
    hidden = (jax.nn.silu(gate_act) * up_act).astype(bf16)
    hidden = flow.tick(hidden)
    down_t = flow.result(f"d{layer}")
    hidden_own, hidden_other = place.relative_rows(hidden)
    result = middle + residual_scale * place.scatter_rows(
        dot(hidden_own, down_t, 1, 1).astype(bf16), dot(hidden_other, down_t, 1, 1).astype(bf16)
    )
    stored = (
        q_low,
        kv_low,
        queries,
        key_rows,
        values,
        log_totals,
        att_low,
        normed_mid,
        inv_mid,
        all_mid,
        gate_act,
        up_act,
        hidden,
    )
    return (result, stored, (q_up, kv_up, out_t, gate, up, down_t))


def layer_backward(
    place, layer, grad_rows, branch_two, weights, before, stored, cosine, sine_table, allowed, gains
):
    q_up, kv_up, out_t, gate, up, down_t = weights
    gain_in, _, q_gain, kv_gain, gain_post = gains
    normed_in, inv_in, all_in, q_normed, q_inverse, kv_normed, kv_inverse = before
    (
        q_low,
        kv_low,
        queries,
        key_rows,
        values,
        log_totals,
        att_low,
        normed_mid,
        inv_mid,
        all_mid,
        gate_act,
        up_act,
        hidden,
    ) = stored
    group_rows = allowed.shape[1]
    heads = q_up.shape[1] // QK
    flow = place.flow

    def in_halves(left, right):
        half = left.shape[1] // 2
        return (
            dot(left[:, half:], right, 0, 0).astype(bf16),
            dot(left[:, :half], right, 0, 0).astype(bf16),
        )

    flow.add(f"grad d{layer}", place.scatter_grad(lambda: in_halves(branch_two, hidden)))
    grad_hidden = dot(branch_two, down_t, 1, 0)
    logistic = jax.nn.sigmoid(gate_act)
    gate_low = (
        grad_hidden * up_act * logistic * (1.0 + gate_act * (1.0 - logistic))
    ).astype(bf16)
    up_low = (grad_hidden * gate_act * logistic).astype(bf16)
    gate_low, up_low = flow.tick(gate_low, up_low)
    gate_own, gate_other = place.relative_rows(gate_low)
    up_own, up_other = place.relative_rows(up_low)
    mid_grad = place.scatter_rows(
        (dot(gate_own, gate, 1, 1) + dot(up_own, up, 1, 1)).astype(bf16),
        (dot(gate_other, gate, 1, 1) + dot(up_other, up, 1, 1)).astype(bf16),
    )
    flow.add(f"grad g{layer}", place.scatter_grad(lambda: in_halves(all_mid, gate_low)))
    flow.add(f"grad u{layer}", place.scatter_grad(lambda: in_halves(all_mid, up_low)))
    mid_grad = flow.tick(mid_grad)
    back_mid, grad_gain_post = norm_back(normed_mid, inv_mid, gain_post, mid_grad)
    grad_middle = grad_rows + back_mid
    branch_one = place.gather_rows((residual_scale * grad_middle).astype(bf16))
    branch_one = flow.tick(branch_one)
    att_grad = dot(branch_one, out_t, 1, 0).astype(bf16).reshape(2, group_rows, heads, VDIM)
    query_grad, key_grad, value_grad = attend_backward(
        queries, key_rows, values, allowed, log_totals, att_grad
    )
    q_full_grad = (
        jnp.concatenate(
            [
                query_grad[..., :NOPE],
                rotate_back(
                    query_grad[..., NOPE:], cosine[:, :, None, :], sine_table[:, :, None, :]
                ),
            ],
            axis=-1,
        )
        .astype(bf16)
        .reshape(2 * group_rows, heads * QK)
    )
    shared_grad = rotate_back(jnp.sum(key_grad[..., NOPE:], axis=2), cosine, sine_table)
    kv_full_grad = (
        jnp.concatenate([key_grad[..., :NOPE], value_grad], axis=-1)
        .astype(bf16)
        .reshape(2 * group_rows, heads * (NOPE + VDIM))
    )
    latent_part = jnp.concatenate(
        [
            dot(q_full_grad, q_up, 1, 1),
            dot(kv_full_grad, kv_up, 1, 1),
            shared_grad.reshape(2 * group_rows, ROPE),
        ],
        axis=1,
    ).astype(bf16)
    latent_part = flow.tick(latent_part)
    latent_grad = place.scatter_rows(*place.relative_rows(latent_part))

    def attention_grads():
        (pack,) = pack_attention(
            [place.to_group(dot(q_low, q_full_grad, 0, 0).astype(bf16), 0)],
            [place.to_group(dot(kv_low, kv_full_grad, 0, 0).astype(bf16), 0)],
            [dot(branch_one, att_low, 0, 0).astype(bf16)],
            place.dp,
        )
        keep, send = jnp.split(pack, 2, axis=0)
        return send, keep

    flow.add(f"grad a{layer}", place.scatter_grad(attention_grads))
    latent_grad = flow.tick(latent_grad)
    down_latent = flow.result(f"w{layer}")
    q_latent_grad, grad_q_gain = norm_back(q_normed, q_inverse, q_gain, latent_grad[:, :QR])
    kv_part_grad, grad_kv_gain = norm_back(
        kv_normed, kv_inverse, kv_gain, latent_grad[:, QR : QR + KVR]
    )
    latent_low = jnp.concatenate(
        [q_latent_grad, kv_part_grad, latent_grad[:, QR + KVR :]], axis=1
    ).astype(bf16)
    in_grad = dot(latent_low, down_latent, 1, 1)
    back_in, grad_gain_in = norm_back(normed_in, inv_in, gain_in, in_grad)
    grad_rows = flow.tick(grad_middle + back_in)
    next_branch = None
    if layer:
        next_branch = place.gather_rows((residual_scale * grad_rows).astype(bf16))
    latent_all = place.gather_rows(latent_low)
    q_width = QR // (2 * place.tensor)
    kv_width = (KVR + ROPE) // (2 * place.tensor)
    share = jnp.where(place.low, 0, place.tensor) + place.column

    def share_grads():
        latent_share = jnp.concatenate(
            [
                lax.dynamic_slice_in_dim(latent_all[:, :QR], share * q_width, q_width, 1),
                lax.dynamic_slice_in_dim(latent_all[:, QR:], share * kv_width, kv_width, 1),
            ],
            axis=1,
        )
        return in_halves(all_in, latent_share)

    def share_steps():
        low, high = yield from place.scatter_grad(share_grads)
        joined = jnp.stack([low, high])
        for bit in (1, 2):
            (taken,) = yield [(joined, "tensor", bit)]
            first = (place.column & bit) == 0
            joined = jnp.stack(
                [jnp.where(first, joined, taken), jnp.where(first, taken, joined)], axis=1
            )
        joined = joined.reshape(2 * place.tensor, *joined.shape[-2:]).swapaxes(0, 1)
        rows = joined.shape[0]
        return joined[..., :q_width].reshape(rows, -1), joined[..., q_width:].reshape(rows, -1)

    flow.add(f"grad s{layer}", share_steps())
    dp = place.dp
    flow.add(
        f"grad gains{layer}",
        place.sum_all(
            jnp.concatenate(
                [
                    place.from_group(grad_gain_in, 0).reshape(dp, -1),
                    grad_q_gain.reshape(dp, -1),
                    grad_kv_gain.reshape(dp, -1),
                    place.from_group(grad_gain_post, 0).reshape(dp, -1),
                ],
                axis=1,
            )
        ),
    )
    return (grad_rows, next_branch)


def pack_attention(q_ups, kv_ups, outs, blocks):
    packs = []
    for q_up, kv_up, out in zip(q_ups, kv_ups, outs):
        columns = kv_up.shape[-1]
        q_up = q_up.reshape(blocks, -1, q_up.shape[-1])
        q_up = jnp.pad(q_up, ((0, 0), (0, 0), (0, columns - q_up.shape[-1])))
        out = out.reshape(blocks, -1, out.shape[-1])
        half = out.shape[1] // 2
        out = jnp.concatenate([out[:, :half], out[:, half:]], axis=2)
        packs.append(
            jnp.concatenate([q_up, kv_up.reshape(blocks, -1, columns), out], axis=1).reshape(
                -1, columns
            )
        )
    return packs


def unpack_attention(pack, blocks, q_rows, kv_rows):
    columns = pack.shape[-1]
    heads = columns // (NOPE + VDIM)
    pack = pack.reshape(blocks, -1, columns)
    q_up = pack[:, :q_rows, : heads * QK].reshape(blocks * q_rows, -1)
    kv_up = pack[:, q_rows : q_rows + kv_rows].reshape(blocks * kv_rows, -1)
    out = pack[:, q_rows + kv_rows :]
    width = heads * VDIM
    out = jnp.concatenate([out[..., :width], out[..., width:]], axis=1).reshape(-1, width)
    return q_up, kv_up, out


def body(
    sizes,
    layer_input,
    doc_ids,
    norm_in,
    q_down,
    q_gain,
    q_up,
    kv_down,
    kv_gain,
    kv_up,
    out_proj,
    norm_post,
    gate_proj,
    up_proj,
    down_proj,
    out_grad,
):
    place = Place(*sizes)
    flow = place.flow
    dp = place.dp

    def halves(array):
        return jnp.split(array, 2, axis=-1)

    q_width = QR // (2 * place.tensor)
    kv_width = (KVR + ROPE) // (2 * place.tensor)

    def share_of(pair):
        share = pair * place.tensor + place.column
        joined = jnp.concatenate(
            [
                lax.dynamic_slice_in_dim(q_down[0], share * q_width, q_width, 1),
                lax.dynamic_slice_in_dim(kv_down[0], share * kv_width, kv_width, 1),
            ],
            axis=1,
        )
        return (joined.astype(f32) * norm_in[0].astype(f32)[:, None]).astype(bf16)

    def doc_steps():
        (taken,) = yield [(doc_ids, "dp", PAIR)]
        return jnp.stack(
            [jnp.where(place.low, doc_ids, taken), jnp.where(place.low, taken, doc_ids)]
        )

    def attention_halves(layer_q_up, layer_kv_up, layer_out):
        return [
            pack_attention(
                [halves(layer_q_up)[pair]], [halves(layer_kv_up)[pair]], [halves(layer_out.T)[pair]], 1
            )[0]
            for pair in range(2)
        ]

    def attention_steps(layer):
        arrays = (q_up[layer], kv_up[layer], out_proj[layer])
        if layer:
            pack = yield from place.gather_weight(attention_halves, *arrays)
        else:
            pack = yield from place.gather_weight(lambda: attention_halves(*arrays))
        layer_q_up, layer_kv_up, layer_out = unpack_attention(
            pack, dp, q_up.shape[1], kv_up.shape[1]
        )
        return place.from_group(layer_q_up, 0), place.from_group(layer_kv_up, 0), layer_out

    flow.add("s", place.gather_weight(lambda: (share_of(0), share_of(1))))
    flow.add("doc", doc_steps())
    flow.add(
        "gains", place.gather_all(jnp.concatenate([norm_in, q_gain, kv_gain, norm_post], axis=1))
    )
    share_rows = q_down.shape[1] // place.tensor
    for layer in range(LAYERS):
        flow.add(f"a{layer}", attention_steps(layer))
        flow.add(f"g{layer}", place.gather_weight(halves, gate_proj[layer]))
        flow.add(f"u{layer}", place.gather_weight(halves, up_proj[layer]))
        flow.add(f"d{layer}", place.gather_weight(lambda a: halves(a.T), down_proj[layer]))
        flow.add(
            f"w{layer}",
            place.gather_whole(
                lax.dynamic_slice_in_dim(
                    jnp.concatenate([q_down[layer], kv_down[layer]], axis=1),
                    place.column * share_rows,
                    share_rows,
                    0,
                )
            ),
        )

    current = place.to_group(layer_input, 1).astype(f32)
    grad_rows = place.to_group(out_grad, 1).astype(f32)
    before = []
    stored = []
    weights = []
    current = flow.tick(current)
    normed_in, inv_in = norm_parts(current)
    all_in = place.gather_rows(normed_in.astype(bf16))
    current = flow.tick(current)
    current = flow.tick(current)
    share = flow.tick(dot(all_in, flow.result("s"), 1, 0).astype(bf16))
    cosine, sine_table, allowed = tables(flow.result("doc"))
    gathered_gains = flow.result("gains").astype(f32)
    widths = [norm_in.shape[1], q_gain.shape[1], kv_gain.shape[1], norm_post.shape[1]]
    starts = [sum(widths[:k]) for k in range(5)]

    def gain_of(layer, position):
        return gathered_gains[:, layer, starts[position] : starts[position + 1]].reshape(-1)

    gains = [
        (
            place.to_group(gain_of(layer, 0), 0),
            None,
            gain_of(layer, 1),
            gain_of(layer, 2),
            place.to_group(gain_of(layer, 3), 0),
        )
        for layer in range(LAYERS)
    ]
    branch = None
    for layer in range(LAYERS):
        if layer == 0:
            latents, kept = first_latents(
                place, place.gather_rows(share, tiled=False), cosine, sine_table, gains[layer]
            )
        else:
            normed_in, inv_in = norm_parts(current)
            low_in = (normed_in * gains[layer][0]).astype(bf16)
            packed, kept = own_latents(
                place, low_in, flow.result(f"w{layer}"), cosine, sine_table, gains[layer]
            )
            packed, low_in = flow.tick(packed, low_in)
            latents = place.gather_rows(packed)
            all_in = place.gather_rows(low_in)
        before.append((normed_in, inv_in, all_in, *kept))
        current, kept, layer_weights = layer_forward(
            place, layer, current, latents, cosine, sine_table, allowed, gains[layer]
        )
        stored.append(kept)
        weights.append(layer_weights)
    branch = place.gather_rows((residual_scale * grad_rows).astype(bf16))
    for layer in reversed(range(LAYERS)):
        if layer < LAYERS - 1:
            branch = flow.tick(branch)
        grad_rows, branch = layer_backward(
            place,
            layer,
            grad_rows,
            branch,
            weights[layer],
            before[layer],
            stored[layer],
            cosine,
            sine_table,
            allowed,
            gains[layer],
        )
    layer_grads = []
    for layer in range(LAYERS):
        grad_q_down, grad_kv_down = (a.astype(f32) for a in flow.result(f"grad s{layer}"))
        if layer == 0:
            scale = norm_in[0].astype(f32)[:, None]
            grad_q_down = grad_q_down * scale
            grad_kv_down = grad_kv_down * scale
        attention_low, attention_high = (
            unpack_attention(a, 1, q_up.shape[1], kv_up.shape[1])
            for a in flow.result(f"grad a{layer}")
        )
        gain_grads = flow.result(f"grad gains{layer}")

        def joined(low, high):
            return jnp.concatenate([low, high], axis=1).astype(f32)

        layer_grads.append(
            (
                grad_q_down,
                joined(attention_low[0], attention_high[0]),
                grad_kv_down,
                joined(attention_low[1], attention_high[1]),
                joined(attention_low[2], attention_high[2]).T,
                joined(*flow.result(f"grad g{layer}")),
                joined(*flow.result(f"grad u{layer}")),
                joined(*flow.result(f"grad d{layer}")).T,
                *[gain_grads[starts[k] : starts[k + 1]] for k in range(4)],
            )
        )
    stacked = [jnp.stack([grads[position] for grads in layer_grads]) for position in range(12)]
    return (
        place.from_group(current.astype(bf16), 1),
        place.from_group(grad_rows.astype(bf16), 1),
        stacked[8],
        stacked[0],
        stacked[9],
        stacked[1],
        stacked[2],
        stacked[10],
        stacked[3],
        stacked[4],
        stacked[11],
        stacked[5],
        stacked[6],
        stacked[7],
    )


def solution(mesh):
    in_specs = (
        P(("dp", "tensor"), None),
        P("dp"),
        P(None, "dp"),
        P(None, "dp", None),
        P(None, "dp"),
        P(None, "dp", "tensor"),
        P(None, "dp", None),
        P(None, "dp"),
        P(None, "dp", "tensor"),
        P(None, "tensor", "dp"),
        P(None, "dp"),
        P(None, "dp", "tensor"),
        P(None, "dp", "tensor"),
        P(None, "tensor", "dp"),
        P(("dp", "tensor"), None),
    )
    out_specs = (
        P(("dp", "tensor"), None),
        P(("dp", "tensor"), None),
        P(None, "dp"),
        P(None, "dp", None),
        P(None, "dp"),
        P(None, "dp", "tensor"),
        P(None, "dp", None),
        P(None, "dp"),
        P(None, "dp", "tensor"),
        P(None, "tensor", "dp"),
        P(None, "dp"),
        P(None, "dp", "tensor"),
        P(None, "dp", "tensor"),
        P(None, "tensor", "dp"),
    )
    sizes = (mesh.shape["dp"], mesh.shape["tensor"])
    return jax.shard_map(
        functools.partial(body, sizes),
        mesh=mesh,
        in_specs=in_specs,
        out_specs=out_specs,
        check_vma=False,
    )
```

```python
import functools
import math

import jax
import jax.numpy as jnp
from jax import lax
from jax.sharding import PartitionSpec as P

NOPE = 64
ROPE = 32
VDIM = 64
QR = 768
KVR = 256
LAYERS = 2
QK = 96

epsilon = 1e-05
residual_scale = 1.4 / math.sqrt(62.0)
rope_base = 10000.0
masked_score = -1e30
bf16 = jnp.bfloat16
f32 = jnp.float32

plan = {
    "doc": (0, 3),
    "gains": (0, 1, 2, 3),
    "s": (0, 1, 2),
    "a0": (0, 1, 3),
    "g0": (1, 2, 3, 5, 6),
    "u0": (2, 4, 5, 6, 7),
    "d0": (3, 4, 6, 7, 8),
    "w1": (2, 3, 4, 5),
    "a1": (5, 6, 7, 9),
    "g1": (5, 6, 9, 11, 12),
    "u1": (6, 7, 11, 12, 13),
    "d1": (6, 7, 12, 13, 14),
    "w0": (12, 13, 14, 15),
    "out": (16, 17, 19, 20),
    "grad d1": (15, 16, 17, 18),
    "grad g1": (16, 17, 18, 19),
    "grad u1": (17, 19, 21, 22),
    "grad a1": (19, 21, 23, 24),
    "grad s1": (21, 22, 23, 24),
    "grad gains1": (20, 21, 22, 23, 24),
    "grad d0": (22, 23, 24, 25),
    "grad g0": (23, 24, 26, 27),
    "grad u0": (24, 26, 28, 29),
    "grad a0": (26, 28, 30, 31),
    "grad s0": (28, 29, 30, 31, 32, 33),
    "grad gains0": (28, 29, 30, 31, 32, 33),
}

PAIR = 2


def dot(left, right, left_dim, right_dim):
    return lax.dot_general(
        left, right, (((left_dim,), (right_dim,)), ((), ())), preferred_element_type=f32
    )


def norm_parts(values):
    inverse = lax.rsqrt(jnp.mean(values * values, axis=-1, keepdims=True) + epsilon)
    return (values * inverse, inverse)


def norm_back(normed, inverse, gain, upstream):
    scaled = upstream * gain
    result = inverse * (scaled - normed * jnp.mean(scaled * normed, axis=-1, keepdims=True))
    return (result, jnp.sum(upstream * normed, axis=0))


def rotate(rotary, cosine, sine_table):
    half_width = rotary.shape[-1] // 2
    first_half = rotary[..., :half_width]
    second_half = rotary[..., half_width:]
    return jnp.concatenate(
        [
            first_half * cosine - second_half * sine_table,
            second_half * cosine + first_half * sine_table,
        ],
        axis=-1,
    )


def rotate_back(upstream, cosine, sine_table):
    return rotate(upstream, cosine, -sine_table)


class Flow:
    def __init__(self, plan, swap):
        self.plan = plan
        self.swap = swap
        self.count = -1
        self.work = {}
        self.due = {}
        self.results = {}

    def add(self, name, steps):
        self.work[name] = (steps, next(steps), None)
        self.due[name] = list(self.plan.get(name, ()))

    def begin(self, name, steps, request):
        moving = [a if axis is None else self.swap(a, axis, bit) for a, axis, bit in request]
        self.work[name] = (steps, None, moving)

    def advance(self, name, steps, arrived):
        try:
            request = steps.send(arrived)
        except StopIteration as end:
            self.results[name] = end.value
            del self.work[name]
            return
        self.begin(name, steps, request)

    def tick(self, *values):
        self.count += 1
        now = []
        for name in self.work:
            due = self.due[name]
            if due and due[0] <= self.count:
                due.pop(0)
                now.append(name)
        held = []
        for name in now:
            _, request, moving = self.work[name]
            held.append([a for a, _, _ in request] if moving is None else moving)
        flat = [a for arrays in held for a in arrays]
        values = list(values)
        if flat:
            out = lax.optimization_barrier((*values, *flat))
            values, flat = list(out[: len(values)]), list(out[len(values) :])
        for name, arrays in zip(now, held):
            tied, flat = flat[: len(arrays)], flat[len(arrays) :]
            steps, request, moving = self.work[name]
            if moving is None:
                self.begin(name, steps, [(a, *r[1:]) for a, r in zip(tied, request)])
            else:
                self.advance(name, steps, tied)
        return values[0] if len(values) == 1 else values

    def result(self, name):
        while name in self.work:
            steps, request, moving = self.work[name]
            if moving is None:
                self.begin(name, steps, request)
            else:
                self.advance(name, steps, moving)
        return self.results[name]


class Place:
    def __init__(self, dp, tensor):
        self.flow = Flow(plan, self.swap)
        self.dp = dp
        self.tensor = tensor
        self.group_bits = [1 << j for j in reversed(range(dp.bit_length() - 1)) if 1 << j != PAIR]
        self.pieces = dp // 2
        self.here = lax.axis_index("dp")
        self.column = lax.axis_index("tensor")
        self.low = (self.here & PAIR) == 0
        self.pairs = [
            [(base | pair * PAIR) * tensor + t for pair in range(2) for t in range(tensor)]
            for base in range(dp)
            if not base & PAIR
        ]

    def swap(self, array, axis, bit):
        size = self.dp if axis == "dp" else self.tensor
        return lax.ppermute(array, axis, [(i, i ^ bit) for i in range(size)])

    def relative(self, piece):
        return sum(bit for j, bit in enumerate(self.group_bits) if piece >> j & 1)

    def order(self):
        return [
            (self.relative(piece) | pair * PAIR)
            for piece in range(self.pieces)
            for pair in range(2)
        ]

    def flip(self, blocks):
        for bit in self.group_bits:
            own = (self.here & bit) != 0
            blocks = [jnp.where(own, blocks[k ^ bit], blocks[k]) for k in range(self.dp)]
        return blocks

    def to_group(self, array, axis):
        blocks = self.flip(jnp.split(array, self.dp, axis=axis))
        return jnp.concatenate([blocks[k] for k in self.order()], axis=axis)

    def from_group(self, array, axis):
        parts = jnp.split(array, self.dp, axis=axis)
        blocks = [None] * self.dp
        for part, k in zip(parts, self.order()):
            blocks[k] = part
        return jnp.concatenate(self.flip(blocks), axis=axis)

    def gather_all(self, array):
        blocks = array[None]
        for j in range(self.dp.bit_length() - 1):
            (taken,) = yield [(blocks, "dp", 1 << j)]
            blocks = jnp.concatenate([blocks, taken], axis=0)
        blocks = [blocks[k] for k in range(self.dp)]
        for j in range(self.dp.bit_length() - 1):
            own = (self.here & (1 << j)) != 0
            blocks = [jnp.where(own, blocks[k ^ (1 << j)], blocks[k]) for k in range(self.dp)]
        return jnp.stack(blocks)

    def gather_weight(self, prepare, *arrays):
        if arrays:
            arrays = yield [(a, None, 0) for a in arrays]
        low, high = prepare(*arrays)
        mine = jnp.where(self.low, low, high)
        (taken,) = yield [(jnp.where(self.low, high, low), "dp", PAIR)]
        pieces = [
            jnp.concatenate(
                [jnp.where(self.low, mine, taken), jnp.where(self.low, taken, mine)], axis=0
            )
        ]
        pieces = yield from self.gather_pieces(pieces)
        return jnp.concatenate(pieces, axis=0)

    def gather_pieces(self, pieces):
        total = len(self.group_bits)
        held = {0: pieces[0]}
        for moves in range(1, total + 1):
            wanted = [k for k in range(1 << total) if k.bit_count() == moves]
            taken = yield [
                (held[k & ~(1 << j)], "dp", self.group_bits[j])
                for k in wanted
                for j in [k.bit_length() - 1]
            ]
            held.update(zip(wanted, taken))
        return [held[k] for k in range(1 << total)]

    def scatter_grad(self, prepare, *arrays):
        if arrays:
            arrays = yield [(a, None, 0) for a in arrays]
        send, keep = prepare(*arrays)
        for bit in reversed(self.group_bits):
            (taken,) = yield [(send, "dp", bit)]
            total = (keep.astype(f32) + taken.astype(f32)).astype(bf16)
            keep, send = jnp.split(total, 2, axis=0)
        (taken,) = yield [(jnp.where(self.low, send, keep), "dp", PAIR)]
        mine = jnp.where(self.low, keep, send)
        return jnp.where(self.low, mine, taken), jnp.where(self.low, taken, mine)

    def gather_whole(self, share):
        (share,) = yield [(share, None, 0)]
        pieces = yield from self.gather_pieces([share])
        joined = self.gather_rows(jnp.concatenate(pieces, axis=0), tiled=False)
        rows, columns = share.shape
        joined = joined.reshape(2, self.tensor, self.pieces, rows, columns)
        return joined.transpose(2, 0, 1, 3, 4).reshape(-1, columns)

    def sum_all(self, blocks):
        blocks = [blocks[k] for k in range(self.dp)]
        bits = [1 << j for j in range(self.dp.bit_length() - 1)]
        for bit in bits:
            own = (self.here & bit) != 0
            blocks = [jnp.where(own, blocks[k ^ bit], blocks[k]) for k in range(self.dp)]
        total = jnp.stack(blocks)
        for bit in reversed(bits):
            half = total.shape[0] // 2
            (taken,) = yield [(total[half:], "dp", bit)]
            total = total[:half] + taken
        for bit in (1, 2):
            (taken,) = yield [(total, "tensor", bit)]
            total = total + taken
        return total[0]

    def gather_rows(self, rows, tiled=True):
        return lax.all_gather(
            rows, ("dp", "tensor"), axis=0, tiled=tiled, axis_index_groups=self.pairs
        )

    def relative_rows(self, rows):
        count = rows.shape[0] // (2 * self.tensor)
        own = jnp.where(self.low, 0, self.tensor) + self.column

        def half(core):
            return jnp.concatenate(
                [
                    lax.dynamic_slice_in_dim(
                        rows, (own ^ (pair * self.tensor + across * 2 + core)) * count, count, 0
                    )
                    for pair in range(2)
                    for across in range(2)
                ],
                axis=0,
            )

        return half(0), half(1)

    def scatter_rows(self, own, other):
        count = own.shape[0] // 4
        half = count // 2
        taken = self.swap(other, "tensor", 1)
        total = (own.astype(f32) + taken.astype(f32)).astype(bf16)
        rows, across, along = total[:count], total[count : 2 * count], total[2 * count : 3 * count]
        corner_first = self.swap(total[3 * count : 3 * count + half], "dp", PAIR)
        corner_second = self.swap(total[3 * count + half :], "tensor", 2)
        across = jnp.concatenate(
            [(across[:half].astype(f32) + corner_first.astype(f32)).astype(bf16), across[half:]],
            axis=0,
        )
        along = jnp.concatenate(
            [along[:half], (along[half:].astype(f32) + corner_second.astype(f32)).astype(bf16)],
            axis=0,
        )
        across = self.swap(across, "tensor", 2)
        along = self.swap(along, "dp", PAIR)
        return rows.astype(f32) + across.astype(f32) + along.astype(f32)

    def scatter_steps(self, own, other):
        count = own.shape[0] // 4
        half = count // 2
        (taken,) = yield [(other, "tensor", 1)]
        total = (own.astype(f32) + taken.astype(f32)).astype(bf16)
        rows, across, along = total[:count], total[count : 2 * count], total[2 * count : 3 * count]
        first, second = yield [
            (total[3 * count : 3 * count + half], "dp", PAIR),
            (total[3 * count + half :], "tensor", 2),
        ]
        across = jnp.concatenate(
            [(across[:half].astype(f32) + first.astype(f32)).astype(bf16), across[half:]], axis=0
        )
        along = jnp.concatenate(
            [along[:half], (along[half:].astype(f32) + second.astype(f32)).astype(bf16)], axis=0
        )
        across, along = yield [(across, "tensor", 2), (along, "dp", PAIR)]
        return rows.astype(f32) + across.astype(f32) + along.astype(f32)

    def own_rows(self, rows):
        count = rows.shape[0] // (2 * self.tensor)
        own = jnp.where(self.low, 0, self.tensor) + self.column
        return lax.dynamic_slice_in_dim(rows, own * count, count, 0)

    def in_order(self, array, axis, bit, place_axis):
        taken = self.swap(array, axis, bit)
        index = self.here if axis == "dp" else self.column
        first = (index & bit) == 0
        return jnp.stack(
            [jnp.where(first, array, taken), jnp.where(first, taken, array)], axis=place_axis
        )


def tables(docs):
    rows_total = docs.shape[1]
    spots = jnp.arange(rows_total, dtype=jnp.int32)
    same = docs[:, :, None] == docs[:, None, :]
    allowed = same & (spots[:, None] >= spots[None, :])
    starts = jnp.sum((docs[:, None, :] < docs[:, :, None]).astype(jnp.int32), axis=-1)
    positions = (spots[None, :] - starts).astype(f32)
    frequency = rope_base ** (-jnp.arange(0, ROPE, 2, dtype=f32) / ROPE)
    angles = positions[..., None] * frequency
    return (jnp.cos(angles), jnp.sin(angles), allowed)


def scores_of(queries, key_rows, allowed):
    scores = jnp.einsum("bqhd,bkhd->bhqk", queries, key_rows, preferred_element_type=f32)
    return jnp.where(allowed[:, None], scores * (1.0 / math.sqrt(QK)), masked_score)


def attend_forward(queries, key_rows, values, allowed):
    scores = scores_of(queries, key_rows, allowed)
    highest = jnp.max(scores, axis=-1, keepdims=True)
    expanded = jnp.exp(scores - highest)
    totals = jnp.sum(expanded, axis=-1, keepdims=True)
    probs_low = (expanded / totals).astype(bf16)
    attended = jnp.einsum("bhqk,bkhd->bqhd", probs_low, values, preferred_element_type=f32)
    return (attended, highest + jnp.log(totals))


def attend_backward(queries, key_rows, values, allowed, log_totals, att_grad):
    scale_factor = 1.0 / math.sqrt(QK)
    probability = jnp.exp(scores_of(queries, key_rows, allowed) - log_totals)
    probs_low = probability.astype(bf16)
    value_grad = jnp.einsum("bhqk,bqhd->bkhd", probs_low, att_grad, preferred_element_type=f32)
    prob_grad = jnp.einsum("bqhd,bkhd->bhqk", att_grad, values, preferred_element_type=f32)
    inner_sum = jnp.sum(prob_grad * probability, axis=-1, keepdims=True)
    score_grad = (probability * (prob_grad - inner_sum)).astype(bf16)
    query_grad = (
        jnp.einsum("bhqk,bkhd->bqhd", score_grad, key_rows, preferred_element_type=f32)
        * scale_factor
    )
    key_grad = (
        jnp.einsum("bhqk,bqhd->bkhd", score_grad, queries, preferred_element_type=f32)
        * scale_factor
    )
    return query_grad, key_grad, value_grad


def rotate_own(place, array, cosine, sine_table):
    flat = (-1, cosine.shape[-1])
    return rotate(
        array, place.own_rows(cosine.reshape(flat)), place.own_rows(sine_table.reshape(flat))
    )


def first_latents(place, shares, cosine, sine_table, gains):
    _, _, q_gain, kv_gain, _ = gains
    width = QR // shares.shape[0]
    rows_total = shares.shape[1]
    q_latent = jnp.swapaxes(shares[..., :width], 0, 1).reshape(rows_total, -1).astype(f32)
    kv_latent = jnp.swapaxes(shares[..., width:], 0, 1).reshape(rows_total, -1).astype(f32)
    q_normed, q_inverse = norm_parts(q_latent)
    kv_normed, kv_inverse = norm_parts(kv_latent[:, :KVR])
    flat = (-1, cosine.shape[-1])
    shared = rotate(kv_latent[:, KVR:], cosine.reshape(flat), sine_table.reshape(flat))
    latents = jnp.concatenate([q_normed * q_gain, kv_normed * kv_gain, shared], axis=1)
    own = [place.own_rows(v) for v in (q_normed, q_inverse, kv_normed, kv_inverse)]
    return latents.astype(bf16), own


def own_latents(place, low_in, down_latent, cosine, sine_table, gains):
    _, _, q_gain, kv_gain, _ = gains
    latent = dot(low_in, down_latent, 1, 0)
    q_normed, q_inverse = norm_parts(latent[:, :QR])
    kv_normed, kv_inverse = norm_parts(latent[:, QR : QR + KVR])
    shared = rotate_own(place, latent[:, QR + KVR :], cosine, sine_table)
    packed = jnp.concatenate([q_normed * q_gain, kv_normed * kv_gain, shared], axis=1).astype(bf16)
    return packed, [q_normed, q_inverse, kv_normed, kv_inverse]


def layer_forward(place, layer, rows_in, latents, cosine, sine_table, allowed, gains):
    flow = place.flow
    gain_post = gains[4]
    group_rows = allowed.shape[1]
    q_up, kv_up, out_t = flow.result(f"a{layer}")
    latents, q_up, kv_up, out_t = flow.tick(latents, q_up, kv_up, out_t)
    heads = q_up.shape[1] // QK
    q_low = latents[:, :QR]
    kv_low = latents[:, QR : QR + KVR]
    q_full = dot(q_low, q_up, 1, 0).reshape(2, group_rows, heads, QK)
    kv_full = dot(kv_low, kv_up, 1, 0).reshape(2, group_rows, heads, NOPE + VDIM)
    queries = jnp.concatenate(
        [
            q_full[..., :NOPE],
            rotate(q_full[..., NOPE:], cosine[:, :, None, :], sine_table[:, :, None, :]),
        ],
        axis=-1,
    ).astype(bf16)
    key_rows = jnp.concatenate(
        [
            kv_full[..., :NOPE].astype(bf16),
            jnp.broadcast_to(
                latents[:, QR + KVR :].reshape(2, group_rows, 1, ROPE),
                (2, group_rows, heads, ROPE),
            ),
        ],
        axis=-1,
    )
    values = kv_full[..., NOPE:].astype(bf16)
    attended, log_totals = attend_forward(queries, key_rows, values, allowed)
    att_low = attended.reshape(2 * group_rows, heads * VDIM).astype(bf16)
    att_low = flow.tick(att_low)
    att_own, att_other = place.relative_rows(att_low)
    middle = rows_in + residual_scale * place.scatter_rows(
        dot(att_own, out_t, 1, 1).astype(bf16), dot(att_other, out_t, 1, 1).astype(bf16)
    )
    middle = flow.tick(middle)
    normed_mid, inv_mid = norm_parts(middle)
    all_mid = place.gather_rows((normed_mid * gain_post).astype(bf16))
    all_mid = flow.tick(all_mid)
    gate = flow.result(f"g{layer}")
    up = flow.result(f"u{layer}")
    gate_act = dot(all_mid, gate, 1, 0)
    up_act = dot(all_mid, up, 1, 0)
    hidden = (jax.nn.silu(gate_act) * up_act).astype(bf16)
    hidden = flow.tick(hidden)
    down_t = flow.result(f"d{layer}")
    hidden_own, hidden_other = place.relative_rows(hidden)
    parts = (
        dot(hidden_own, down_t, 1, 1).astype(bf16),
        dot(hidden_other, down_t, 1, 1).astype(bf16),
    )
    if layer < LAYERS - 1:
        result = middle + residual_scale * place.scatter_rows(*parts)
    else:
        flow.add("out", place.scatter_steps(*parts))
        result = middle
    stored = (
        q_low,
        kv_low,
        queries,
        key_rows,
        values,
        log_totals,
        att_low,
        normed_mid,
        inv_mid,
        all_mid,
        gate_act,
        up_act,
        hidden,
    )
    return (result, stored, (q_up, kv_up, out_t, gate, up, down_t))


def layer_backward(
    place, layer, grad_rows, branch_two, weights, before, stored, cosine, sine_table, allowed, gains
):
    q_up, kv_up, out_t, gate, up, down_t = weights
    gain_in, _, q_gain, kv_gain, gain_post = gains
    normed_in, inv_in, all_in, q_normed, q_inverse, kv_normed, kv_inverse = before
    (
        q_low,
        kv_low,
        queries,
        key_rows,
        values,
        log_totals,
        att_low,
        normed_mid,
        inv_mid,
        all_mid,
        gate_act,
        up_act,
        hidden,
    ) = stored
    group_rows = allowed.shape[1]
    heads = q_up.shape[1] // QK
    flow = place.flow

    def in_halves(left, right):
        half = left.shape[1] // 2
        return (
            dot(left[:, half:], right, 0, 0).astype(bf16),
            dot(left[:, :half], right, 0, 0).astype(bf16),
        )

    flow.add(f"grad d{layer}", place.scatter_grad(lambda: in_halves(branch_two, hidden)))
    grad_hidden = dot(branch_two, down_t, 1, 0)
    logistic = jax.nn.sigmoid(gate_act)
    gate_low = (
        grad_hidden * up_act * logistic * (1.0 + gate_act * (1.0 - logistic))
    ).astype(bf16)
    up_low = (grad_hidden * gate_act * logistic).astype(bf16)
    gate_low, up_low = flow.tick(gate_low, up_low)
    gate_own, gate_other = place.relative_rows(gate_low)
    up_own, up_other = place.relative_rows(up_low)
    mid_grad = place.scatter_rows(
        (dot(gate_own, gate, 1, 1) + dot(up_own, up, 1, 1)).astype(bf16),
        (dot(gate_other, gate, 1, 1) + dot(up_other, up, 1, 1)).astype(bf16),
    )
    flow.add(f"grad g{layer}", place.scatter_grad(lambda: in_halves(all_mid, gate_low)))
    flow.add(f"grad u{layer}", place.scatter_grad(lambda: in_halves(all_mid, up_low)))
    mid_grad = flow.tick(mid_grad)
    back_mid, grad_gain_post = norm_back(normed_mid, inv_mid, gain_post, mid_grad)
    grad_middle = grad_rows + back_mid
    branch_one = place.gather_rows((residual_scale * grad_middle).astype(bf16))
    branch_one = flow.tick(branch_one)
    att_grad = dot(branch_one, out_t, 1, 0).astype(bf16).reshape(2, group_rows, heads, VDIM)
    query_grad, key_grad, value_grad = attend_backward(
        queries, key_rows, values, allowed, log_totals, att_grad
    )
    q_full_grad = (
        jnp.concatenate(
            [
                query_grad[..., :NOPE],
                rotate_back(
                    query_grad[..., NOPE:], cosine[:, :, None, :], sine_table[:, :, None, :]
                ),
            ],
            axis=-1,
        )
        .astype(bf16)
        .reshape(2 * group_rows, heads * QK)
    )
    shared_grad = rotate_back(jnp.sum(key_grad[..., NOPE:], axis=2), cosine, sine_table)
    kv_full_grad = (
        jnp.concatenate([key_grad[..., :NOPE], value_grad], axis=-1)
        .astype(bf16)
        .reshape(2 * group_rows, heads * (NOPE + VDIM))
    )
    latent_part = jnp.concatenate(
        [
            dot(q_full_grad, q_up, 1, 1),
            dot(kv_full_grad, kv_up, 1, 1),
            shared_grad.reshape(2 * group_rows, ROPE),
        ],
        axis=1,
    ).astype(bf16)
    latent_part = flow.tick(latent_part)
    latent_grad = place.scatter_rows(*place.relative_rows(latent_part))

    def attention_grads():
        (pack,) = pack_attention(
            [place.to_group(dot(q_low, q_full_grad, 0, 0).astype(bf16), 0)],
            [place.to_group(dot(kv_low, kv_full_grad, 0, 0).astype(bf16), 0)],
            [dot(branch_one, att_low, 0, 0).astype(bf16)],
            place.dp,
        )
        keep, send = jnp.split(pack, 2, axis=0)
        return send, keep

    flow.add(f"grad a{layer}", place.scatter_grad(attention_grads))
    latent_grad = flow.tick(latent_grad)
    down_latent = flow.result(f"w{layer}")
    q_latent_grad, grad_q_gain = norm_back(q_normed, q_inverse, q_gain, latent_grad[:, :QR])
    kv_part_grad, grad_kv_gain = norm_back(
        kv_normed, kv_inverse, kv_gain, latent_grad[:, QR : QR + KVR]
    )
    latent_low = jnp.concatenate(
        [q_latent_grad, kv_part_grad, latent_grad[:, QR + KVR :]], axis=1
    ).astype(bf16)
    in_grad = dot(latent_low, down_latent, 1, 1)
    back_in, grad_gain_in = norm_back(normed_in, inv_in, gain_in, in_grad)
    grad_rows = flow.tick(grad_middle + back_in)
    next_branch = None
    if layer:
        next_branch = place.gather_rows((residual_scale * grad_rows).astype(bf16))
    latent_all = place.gather_rows(latent_low)
    q_width = QR // (2 * place.tensor)
    kv_width = (KVR + ROPE) // (2 * place.tensor)
    share = jnp.where(place.low, 0, place.tensor) + place.column

    def share_grads():
        latent_share = jnp.concatenate(
            [
                lax.dynamic_slice_in_dim(latent_all[:, :QR], share * q_width, q_width, 1),
                lax.dynamic_slice_in_dim(latent_all[:, QR:], share * kv_width, kv_width, 1),
            ],
            axis=1,
        )
        return in_halves(all_in, latent_share)

    def share_steps():
        low, high = yield from place.scatter_grad(share_grads)
        joined = jnp.stack([low, high])
        for bit in (1, 2):
            (taken,) = yield [(joined, "tensor", bit)]
            first = (place.column & bit) == 0
            joined = jnp.stack(
                [jnp.where(first, joined, taken), jnp.where(first, taken, joined)], axis=1
            )
        joined = joined.reshape(2 * place.tensor, *joined.shape[-2:]).swapaxes(0, 1)
        rows = joined.shape[0]
        return joined[..., :q_width].reshape(rows, -1), joined[..., q_width:].reshape(rows, -1)

    flow.add(f"grad s{layer}", share_steps())
    dp = place.dp
    flow.add(
        f"grad gains{layer}",
        place.sum_all(
            jnp.concatenate(
                [
                    place.from_group(grad_gain_in, 0).reshape(dp, -1),
                    grad_q_gain.reshape(dp, -1),
                    grad_kv_gain.reshape(dp, -1),
                    place.from_group(grad_gain_post, 0).reshape(dp, -1),
                ],
                axis=1,
            )
        ),
    )
    return (grad_rows, next_branch)


def pack_attention(q_ups, kv_ups, outs, blocks):
    packs = []
    for q_up, kv_up, out in zip(q_ups, kv_ups, outs):
        columns = kv_up.shape[-1]
        q_up = q_up.reshape(blocks, -1, q_up.shape[-1])
        q_up = jnp.pad(q_up, ((0, 0), (0, 0), (0, columns - q_up.shape[-1])))
        out = out.reshape(blocks, -1, out.shape[-1])
        half = out.shape[1] // 2
        out = jnp.concatenate([out[:, :half], out[:, half:]], axis=2)
        packs.append(
            jnp.concatenate([q_up, kv_up.reshape(blocks, -1, columns), out], axis=1).reshape(
                -1, columns
            )
        )
    return packs


def unpack_attention(pack, blocks, q_rows, kv_rows):
    columns = pack.shape[-1]
    heads = columns // (NOPE + VDIM)
    pack = pack.reshape(blocks, -1, columns)
    q_up = pack[:, :q_rows, : heads * QK].reshape(blocks * q_rows, -1)
    kv_up = pack[:, q_rows : q_rows + kv_rows].reshape(blocks * kv_rows, -1)
    out = pack[:, q_rows + kv_rows :]
    width = heads * VDIM
    out = jnp.concatenate([out[..., :width], out[..., width:]], axis=1).reshape(-1, width)
    return q_up, kv_up, out


def body(
    sizes,
    layer_input,
    doc_ids,
    norm_in,
    q_down,
    q_gain,
    q_up,
    kv_down,
    kv_gain,
    kv_up,
    out_proj,
    norm_post,
    gate_proj,
    up_proj,
    down_proj,
    out_grad,
):
    place = Place(*sizes)
    flow = place.flow
    dp = place.dp

    def halves(array):
        return jnp.split(array, 2, axis=-1)

    q_width = QR // (2 * place.tensor)
    kv_width = (KVR + ROPE) // (2 * place.tensor)

    def share_of(pair):
        share = pair * place.tensor + place.column
        joined = jnp.concatenate(
            [
                lax.dynamic_slice_in_dim(q_down[0], share * q_width, q_width, 1),
                lax.dynamic_slice_in_dim(kv_down[0], share * kv_width, kv_width, 1),
            ],
            axis=1,
        )
        return (joined.astype(f32) * norm_in[0].astype(f32)[:, None]).astype(bf16)

    def doc_steps():
        (taken,) = yield [(doc_ids, "dp", PAIR)]
        return jnp.stack(
            [jnp.where(place.low, doc_ids, taken), jnp.where(place.low, taken, doc_ids)]
        )

    def attention_halves(layer_q_up, layer_kv_up, layer_out):
        return [
            pack_attention(
                [halves(layer_q_up)[pair]], [halves(layer_kv_up)[pair]], [halves(layer_out.T)[pair]], 1
            )[0]
            for pair in range(2)
        ]

    def attention_steps(layer):
        arrays = (q_up[layer], kv_up[layer], out_proj[layer])
        if layer:
            pack = yield from place.gather_weight(attention_halves, *arrays)
        else:
            pack = yield from place.gather_weight(lambda: attention_halves(*arrays))
        layer_q_up, layer_kv_up, layer_out = unpack_attention(
            pack, dp, q_up.shape[1], kv_up.shape[1]
        )
        return place.from_group(layer_q_up, 0), place.from_group(layer_kv_up, 0), layer_out

    flow.add("s", place.gather_weight(lambda: (share_of(0), share_of(1))))
    flow.add("doc", doc_steps())
    flow.add(
        "gains", place.gather_all(jnp.concatenate([norm_in, q_gain, kv_gain, norm_post], axis=1))
    )
    share_rows = q_down.shape[1] // place.tensor
    for layer in range(LAYERS):
        flow.add(f"a{layer}", attention_steps(layer))
        flow.add(f"g{layer}", place.gather_weight(halves, gate_proj[layer]))
        flow.add(f"u{layer}", place.gather_weight(halves, up_proj[layer]))
        flow.add(f"d{layer}", place.gather_weight(lambda a: halves(a.T), down_proj[layer]))
        flow.add(
            f"w{layer}",
            place.gather_whole(
                lax.dynamic_slice_in_dim(
                    jnp.concatenate([q_down[layer], kv_down[layer]], axis=1),
                    place.column * share_rows,
                    share_rows,
                    0,
                )
            ),
        )

    current = place.to_group(layer_input, 1).astype(f32)
    grad_rows = place.to_group(out_grad, 1).astype(f32)
    before = []
    stored = []
    weights = []
    current = flow.tick(current)
    normed_in, inv_in = norm_parts(current)
    all_in = place.gather_rows(normed_in.astype(bf16))
    current = flow.tick(current)
    current = flow.tick(current)
    share = flow.tick(dot(all_in, flow.result("s"), 1, 0).astype(bf16))
    cosine, sine_table, allowed = tables(flow.result("doc"))
    gathered_gains = flow.result("gains").astype(f32)
    widths = [norm_in.shape[1], q_gain.shape[1], kv_gain.shape[1], norm_post.shape[1]]
    starts = [sum(widths[:k]) for k in range(5)]

    def gain_of(layer, position):
        return gathered_gains[:, layer, starts[position] : starts[position + 1]].reshape(-1)

    gains = [
        (
            place.to_group(gain_of(layer, 0), 0),
            None,
            gain_of(layer, 1),
            gain_of(layer, 2),
            place.to_group(gain_of(layer, 3), 0),
        )
        for layer in range(LAYERS)
    ]
    branch = None
    for layer in range(LAYERS):
        if layer == 0:
            latents, kept = first_latents(
                place, place.gather_rows(share, tiled=False), cosine, sine_table, gains[layer]
            )
        else:
            normed_in, inv_in = norm_parts(current)
            low_in = (normed_in * gains[layer][0]).astype(bf16)
            packed, kept = own_latents(
                place, low_in, flow.result(f"w{layer}"), cosine, sine_table, gains[layer]
            )
            packed, low_in = flow.tick(packed, low_in)
            latents = place.gather_rows(packed)
            all_in = place.gather_rows(low_in)
        before.append((normed_in, inv_in, all_in, *kept))
        current, kept, layer_weights = layer_forward(
            place, layer, current, latents, cosine, sine_table, allowed, gains[layer]
        )
        stored.append(kept)
        weights.append(layer_weights)
    branch = place.gather_rows((residual_scale * grad_rows).astype(bf16))
    for layer in reversed(range(LAYERS)):
        if layer < LAYERS - 1:
            branch = flow.tick(branch)
        grad_rows, branch = layer_backward(
            place,
            layer,
            grad_rows,
            branch,
            weights[layer],
            before[layer],
            stored[layer],
            cosine,
            sine_table,
            allowed,
            gains[layer],
        )
    for _ in range(28, 34):
        grad_rows = flow.tick(grad_rows)
    current = current + residual_scale * flow.result("out")
    layer_grads = []
    for layer in range(LAYERS):
        grad_q_down, grad_kv_down = (a.astype(f32) for a in flow.result(f"grad s{layer}"))
        if layer == 0:
            scale = norm_in[0].astype(f32)[:, None]
            grad_q_down = grad_q_down * scale
            grad_kv_down = grad_kv_down * scale
        attention_low, attention_high = (
            unpack_attention(a, 1, q_up.shape[1], kv_up.shape[1])
            for a in flow.result(f"grad a{layer}")
        )
        gain_grads = flow.result(f"grad gains{layer}")

        def joined(low, high):
            return jnp.concatenate([low, high], axis=1).astype(f32)

        layer_grads.append(
            (
                grad_q_down,
                joined(attention_low[0], attention_high[0]),
                grad_kv_down,
                joined(attention_low[1], attention_high[1]),
                joined(attention_low[2], attention_high[2]).T,
                joined(*flow.result(f"grad g{layer}")),
                joined(*flow.result(f"grad u{layer}")),
                joined(*flow.result(f"grad d{layer}")).T,
                *[gain_grads[starts[k] : starts[k + 1]] for k in range(4)],
            )
        )
    stacked = [jnp.stack([grads[position] for grads in layer_grads]) for position in range(12)]
    return (
        place.from_group(current.astype(bf16), 1),
        place.from_group(grad_rows.astype(bf16), 1),
        stacked[8],
        stacked[0],
        stacked[9],
        stacked[1],
        stacked[2],
        stacked[10],
        stacked[3],
        stacked[4],
        stacked[11],
        stacked[5],
        stacked[6],
        stacked[7],
    )


def solution(mesh):
    in_specs = (
        P(("dp", "tensor"), None),
        P("dp"),
        P(None, "dp"),
        P(None, "dp", None),
        P(None, "dp"),
        P(None, "dp", "tensor"),
        P(None, "dp", None),
        P(None, "dp"),
        P(None, "dp", "tensor"),
        P(None, "tensor", "dp"),
        P(None, "dp"),
        P(None, "dp", "tensor"),
        P(None, "dp", "tensor"),
        P(None, "tensor", "dp"),
        P(("dp", "tensor"), None),
    )
    out_specs = (
        P(("dp", "tensor"), None),
        P(("dp", "tensor"), None),
        P(None, "dp"),
        P(None, "dp", None),
        P(None, "dp"),
        P(None, "dp", "tensor"),
        P(None, "dp", None),
        P(None, "dp"),
        P(None, "dp", "tensor"),
        P(None, "tensor", "dp"),
        P(None, "dp"),
        P(None, "dp", "tensor"),
        P(None, "dp", "tensor"),
        P(None, "tensor", "dp"),
    )
    sizes = (mesh.shape["dp"], mesh.shape["tensor"])
    return jax.shard_map(
        functools.partial(body, sizes),
        mesh=mesh,
        in_specs=in_specs,
        out_specs=out_specs,
        check_vma=False,
    )
```
